256 devices in a mesh: row: 32 (over z, y_hi, core), col: 8 (over y_lo, x).
Axes of the slice: x: 4, y: 4 (y_hi: 2, y_lo: 2; y = y_hi * 2 + y_lo), z: 8, core: 2. Of those that a mesh axis runs over, the one named last changes fastest.
Arguments:
- vectors: float32 [8, 131072], P(None, ('row', 'col')), may hold values from -6 to 6
- tiles: float32 [32, 384, 128, 128], P('row', 'col'), may hold values from -0.1875 to 0.1875
- tile_rows: int32 [32, 384], P('row', 'col'), may hold values from 0 to 31
- tile_cols: int32 [32, 384], P('row', 'col'), may hold values from 0 to 31, as said below
- counts: int32 [32, 8], P('row', 'col'), may hold values from 1 to 48, as said below
Outputs:
- product: float32 [8, 131072], P(None, ('row', 'col'))
The draws below stay inside these ranges and needn't reach their ends.
Inputs may be any that keep to these rules, and one draw needn't show every extreme that they name: `tile_cols`: on grid positions with c = 0 each tile's column is at most its row. `counts`: some grid position holds exactly 48 live tiles.
All inputs are finite; a program needn't handle non-finite values.
Results may differ from the reference program's by a relative error of at most 0.0003.
Values sent between devices are 32-bit elements; how exact they have to be, the bound alone decides.
No kernel may reach another device: no remote copies, remote signals or barrier semaphores. Data moves between devices by JAX's collectives and lax.ppermute only.
A program may use at most 64 MiB of HBM per device.

```python
import jax
import jax.numpy as jnp
from jax import lax

TILE = 128
COLS = 8
BLK_SEG = 32
TILES_DEV = 48
SEG = 4096
NROWS = 131072
N_ROW = 32
N_COL = 8


def pattern_pair(key):
    shape = (N_ROW, N_COL * TILES_DEV)
    rows = jax.random.randint(jax.random.fold_in(key, 11), shape, 0, BLK_SEG)
    cols = jax.random.randint(jax.random.fold_in(key, 12), shape, 0, BLK_SEG)
    grid_col = jnp.arange(N_COL * TILES_DEV, dtype=jnp.int32) // TILES_DEV
    first = (grid_col == 0)[None, :]
    cols = jnp.where(first, jnp.minimum(cols, rows), cols)
    return (rows.astype(jnp.int32), cols.astype(jnp.int32))


def draw_tile_rows(key, part):
    rows, cols = pattern_pair(key)
    return rows


def draw_tile_cols(key, part):
    rows, cols = pattern_pair(key)
    return cols


def draw_counts(key, part):
    key = jax.random.fold_in(key, 5)
    base = jax.random.randint(jax.random.fold_in(key, 1), (N_ROW * N_COL,), 0, TILES_DEV + 1)
    loads = jnp.maximum(1, base * base // TILES_DEV)
    where_full = jax.random.randint(jax.random.fold_in(key, 2), (), 0, N_ROW * N_COL)
    loads = jnp.where(jnp.arange(N_ROW * N_COL) == where_full, TILES_DEV, loads)
    return loads.reshape(N_ROW, N_COL).astype(jnp.int32)


def steps_of(key, dims, pieces, low, top_value):
    def one(position, blocks):
        heights = jax.random.uniform(jax.random.fold_in(jax.random.fold_in(key, 6), position), (blocks,), jnp.float32, low / len(pieces), top_value / len(pieces))
        return jnp.repeat(jnp.exp(heights), dims[position] // blocks).reshape((-1,) + (1,) * (len(dims) - position - 1))

    factor_of = one(*pieces[0])
    for cut in pieces[1:]:
        factor_of = factor_of * one(*cut)
    return factor_of


def gaussian(own_key, dims, spread, bound, shards=(), kind=jnp.bfloat16):
    values = jax.random.normal(own_key, dims, jnp.float32) * spread
    if len(shards) > 0:
        values = steps_of(own_key, dims, shards, -0.22, 0.18) * values
    return jnp.clip(values, min=-bound, max=bound).astype(kind)


def setup_inputs(seed: int = 0) -> dict:
    splits = jax.random.split(jax.random.key(seed), 6)
    return {
        "vectors": gaussian(splits[0], (COLS, NROWS), 1.0, 6.0, ((1, 256),), jnp.float32),
        "tiles": gaussian(splits[1], (N_ROW, N_COL * TILES_DEV, TILE, TILE), 1024 ** -0.5, 0.1875, ((0, 32), (1, 8)), jnp.float32),
        "tile_rows": draw_tile_rows(jax.random.fold_in(splits[5], 71), 0),
        "tile_cols": draw_tile_cols(jax.random.fold_in(splits[5], 71), 0),
        "counts": draw_counts(jax.random.fold_in(splits[5], 71), 0),
    }


def reference(vectors, tiles, tile_rows, tile_cols, counts):
    num_rows = tile_rows.shape[0]
    slots = tile_rows.shape[1] // N_COL
    blocks = vectors.reshape(COLS, num_rows * BLK_SEG, TILE)
    tiles_all = tiles.reshape(num_rows * N_COL, slots, TILE, TILE)
    rows_all = tile_rows.reshape(num_rows * N_COL, slots)
    cols_all = tile_cols.reshape(num_rows * N_COL, slots)
    count_all = counts.reshape(num_rows * N_COL)
    places = jnp.arange(num_rows * N_COL, dtype=jnp.int32)

    def step(carry, item):
        place, tile_set, rows_loc, cols_loc, live_count = item
        grid_row = place // N_COL
        grid_col = place % N_COL
        glob_rows = (grid_row * BLK_SEG + rows_loc).astype(jnp.int32)
        glob_cols = (((grid_row - grid_col) % num_rows) * BLK_SEG + cols_loc).astype(jnp.int32)
        live = (jnp.arange(slots, dtype=jnp.int32) < live_count).astype(jnp.float32)
        inbound = blocks[:, glob_cols, :]
        plain = jnp.einsum("ckj,kij->cki", inbound, tile_set, precision=lax.Precision.HIGHEST)
        plain = plain * live[None, :, None]
        rowside = blocks[:, glob_rows, :]
        mirror = jnp.einsum("cki,kij->ckj", rowside, tile_set, precision=lax.Precision.HIGHEST)
        mirror = mirror * live[None, :, None]
        carry = carry.at[:, glob_rows, :].add(plain)
        carry = carry.at[:, glob_cols, :].add(mirror)
        return carry, None

    start = jnp.zeros((COLS, num_rows * BLK_SEG, TILE), jnp.float32)
    total, _ = lax.scan(step, start, (places, tiles_all, rows_all, cols_all, count_all))
    return total.reshape(COLS, num_rows * SEG)
```

```python
import functools

import jax
import jax.numpy as jnp
from jax import lax
from jax.experimental import pallas as pl
from jax.experimental.pallas import tpu as pltpu
from jax.sharding import PartitionSpec as P

TILE = 128
AXES = ("row", "col")


def split(x):
    hi = x.astype(jnp.bfloat16)
    return hi, x - hi.astype(jnp.float32)


def tiles_kernel(transposed, count_ref, from_ref, to_ref, seg_ref, tiles_ref, out_ref):
    slots = tiles_ref.shape[1]
    width = seg_ref.shape[1]
    dims = (((1,), (1 if transposed else 0,)), ((), ()))
    out_ref[...] = jnp.zeros_like(out_ref)
    for t in range(slots):
        live = t < count_ref[0, 0]
        vec = jnp.where(live, seg_ref[from_ref[0, t]], 0.0)
        vec_hi, vec_lo = split(vec)
        both = jnp.concatenate([vec_hi.astype(jnp.float32), vec_lo], axis=0).astype(jnp.bfloat16)
        tile_hi, tile_lo = split(tiles_ref[0, t])
        main = lax.dot_general(both, tile_hi, dims, preferred_element_type=jnp.float32)
        rest = lax.dot_general(both, tile_lo.astype(jnp.bfloat16), dims, preferred_element_type=jnp.float32)
        to = to_ref[0, t]
        out_ref[to] = out_ref[to] + (main[:width] + (main[width:] + rest[:width]))


def apply_tiles(transposed, seg, tiles, come_from, go_to, counts):
    smem = pl.BlockSpec(memory_space=pltpu.SMEM)
    vmem = pl.BlockSpec(memory_space=pltpu.VMEM)
    slots = tiles.shape[1]
    return pl.pallas_call(
        functools.partial(tiles_kernel, transposed),
        out_shape=jax.ShapeDtypeStruct(seg.shape, jnp.float32),
        in_specs=[smem, smem, smem, vmem, vmem],
        out_specs=vmem,
        compiler_params=pltpu.CompilerParams(vmem_limit_bytes=32 * 2**20),
        cost_estimate=pl.CostEstimate(
            flops=2 * 4 * slots * 8 * TILE * TILE, bytes_accessed=slots * TILE * TILE * 4, transcendentals=0
        ),
    )(counts, come_from, go_to, seg, tiles)


def local(vectors, tiles, tile_rows, tile_cols, counts):
    nrow, ncol = lax.axis_size("row"), lax.axis_size("col")
    width, piece_len = vectors.shape
    per = piece_len // TILE

    def place(r, c):
        return (r % nrow) * ncol + c

    onward = [(place(r, c), place(r + c, c)) for r in range(nrow) for c in range(ncol)]
    piece = vectors.reshape(width, per, TILE).transpose(1, 0, 2)
    own = lax.all_to_all(
        jnp.broadcast_to(piece[None], (ncol, per, width, TILE)), "col", split_axis=0, concat_axis=0, tiled=True
    )
    own_seg = own.reshape(ncol * per, width, TILE)
    other_seg = lax.ppermute(own_seg, AXES, onward)
    col_part = apply_tiles(False, own_seg, tiles, tile_rows, tile_cols, counts)
    home = lax.ppermute(col_part, AXES, [(b, a) for a, b in onward])
    row_part = apply_tiles(True, other_seg, tiles, tile_cols, tile_rows, counts)
    total = (row_part + home).reshape(ncol, per, width, TILE)
    parts = lax.all_to_all(total, "col", split_axis=0, concat_axis=0, tiled=True)
    return parts.sum(axis=0).transpose(1, 0, 2).reshape(width, piece_len)


def solution(mesh):
    placed = (
        P(None, AXES),
        P("row", "col", None, None),
        P("row", "col"),
        P("row", "col"),
        P("row", "col"),
    )
    return jax.shard_map(local, mesh=mesh, in_specs=placed, out_specs=P(None, AXES), check_vma=False)
```

```python
import functools

import jax
import jax.numpy as jnp
from jax import lax
from jax.experimental import pallas as pl
from jax.experimental.pallas import tpu as pltpu
from jax.sharding import PartitionSpec as P

TILE = 128
AXES = ("row", "col")
SMEM = pl.BlockSpec(memory_space=pltpu.SMEM)
VMEM = pl.BlockSpec(memory_space=pltpu.VMEM)


def split(x):
    hi = x.astype(jnp.bfloat16)
    return hi, (x - hi.astype(jnp.float32)).astype(jnp.bfloat16)


def stage_kernel(*refs):
    vec_ref, *sources = refs[:5]
    copies_ref, *targets = refs[5:10]
    sems = refs[10]
    ncol = copies_ref.shape[0]
    moves = [pltpu.make_async_copy(vec_ref, copies_ref.at[k], sems.at[k]) for k in range(ncol)]
    moves += [
        pltpu.make_async_copy(s, t, sems.at[ncol + n]) for n, (s, t) in enumerate(zip(sources, targets, strict=True))
    ]
    for move in moves:
        move.start()
    for move in moves:
        move.wait()


def stage(vectors, tiles, tile_rows, tile_cols, counts, ncol):
    rest = [tiles, tile_rows, tile_cols, counts]
    return pl.pallas_call(
        stage_kernel,
        out_shape=[pltpu.VMEM((ncol, *vectors.shape), vectors.dtype), pltpu.VMEM(tiles.shape, tiles.dtype)]
        + [pltpu.SMEM(a.shape, a.dtype) for a in rest[1:]],
        in_specs=[pl.BlockSpec(memory_space=pltpu.HBM)] * 5,
        out_specs=[VMEM, VMEM, SMEM, SMEM, SMEM],
        scratch_shapes=[pltpu.SemaphoreType.DMA((ncol + 4,))],
        cost_estimate=pl.CostEstimate(flops=0, bytes_accessed=tiles.size * 4, transcendentals=0),
    )(vectors, *rest)


def tiles_kernel(mirrored, count_ref, rows_ref, cols_ref, seg_ref, tiles_ref, out_ref):
    slots = tiles_ref.shape[1]
    width = seg_ref.shape[1]
    dims = (((1,), (0 if mirrored else 1,)), ((), ()))
    out_ref[...] = jnp.zeros_like(out_ref)
    for t in range(slots):
        row, col = rows_ref[0, t], cols_ref[0, t]
        vec = jnp.where(t < count_ref[0, 0], seg_ref[row if mirrored else col], 0.0)
        hi = vec.astype(jnp.bfloat16).astype(jnp.float32)
        both = jnp.concatenate([hi, vec - hi], axis=0).astype(jnp.bfloat16)
        tile_hi, tile_lo = split(tiles_ref[0, t])
        main = lax.dot_general(both, tile_hi, dims, preferred_element_type=jnp.float32)
        rest = lax.dot_general(both, tile_lo, dims, preferred_element_type=jnp.float32)
        to = col if mirrored else row
        out_ref[to] = out_ref[to] + (main[:width] + (main[width:] + rest[:width]))


def apply_tiles(mirrored, seg, tiles, tile_rows, tile_cols, counts):
    slots = tiles.shape[1]
    return pl.pallas_call(
        functools.partial(tiles_kernel, mirrored),
        out_shape=jax.ShapeDtypeStruct(seg.shape, jnp.float32),
        in_specs=[SMEM, SMEM, SMEM, VMEM, VMEM],
        out_specs=VMEM,
        compiler_params=pltpu.CompilerParams(vmem_limit_bytes=32 * 2**20),
        cost_estimate=pl.CostEstimate(
            flops=2 * 4 * slots * 8 * TILE * TILE, bytes_accessed=slots * TILE * TILE * 4, transcendentals=0
        ),
    )(counts, tile_rows, tile_cols, seg, tiles)


def local(vectors, tiles, tile_rows, tile_cols, counts):
    nrow, ncol = lax.axis_size("row"), lax.axis_size("col")
    width, piece_len = vectors.shape
    per = piece_len // TILE

    def place(r, c):
        return (r % nrow) * ncol + c

    onward = [(place(r, (c + ncol // 2) % ncol), place(r + c, c)) for r in range(nrow) for c in range(ncol)]
    piece = vectors.reshape(width, per, TILE).transpose(1, 0, 2)
    copies, *data = stage(piece, tiles, tile_rows, tile_cols, counts, ncol)
    own = lax.all_to_all(copies, "col", split_axis=0, concat_axis=0, tiled=True)
    own_seg = own.reshape(ncol * per, width, TILE)
    other_seg = lax.ppermute(own_seg, AXES, onward)
    col_part = apply_tiles(True, own_seg, *data)
    home = lax.ppermute(col_part, AXES, [(b, a) for a, b in onward])
    row_part = apply_tiles(False, other_seg, *data)
    total = (row_part + home).reshape(ncol, per, width, TILE)
    pieces = lax.all_to_all(total, "col", split_axis=0, concat_axis=0, tiled=True)
    return pieces.sum(axis=0).transpose(1, 0, 2).reshape(width, piece_len)


def solution(mesh):
    placed = (
        P(None, AXES),
        P("row", "col", None, None),
        P("row", "col"),
        P("row", "col"),
        P("row", "col"),
    )
    return jax.shard_map(local, mesh=mesh, in_specs=placed, out_specs=P(None, AXES), check_vma=False)
```

```python
import functools

import jax
import jax.numpy as jnp
from jax import lax
from jax.experimental import pallas as pl
from jax.experimental.pallas import tpu as pltpu
from jax.sharding import PartitionSpec as P

TILE = 128
CHUNKS = 4
AXES = ("row", "col")
SMEM = pl.BlockSpec(memory_space=pltpu.SMEM)
VMEM = pl.BlockSpec(memory_space=pltpu.VMEM)


def split(x):
    hi = x.astype(jnp.bfloat16)
    return hi, (x - hi.astype(jnp.float32)).astype(jnp.bfloat16)


def move_all(sources, targets, sems):
    moves = [pltpu.make_async_copy(s, t, sems.at[n]) for n, (s, t) in enumerate(zip(sources, targets, strict=True))]
    for move in moves:
        move.start()
    for move in moves:
        move.wait()


def stage_kernel(*refs):
    half = len(refs) // 2
    sources, targets = list(refs[:half]), list(refs[half:-1])
    chunk = sources[0].shape[1] // CHUNKS
    parts = [(0, pl.ds(n * chunk, chunk)) for n in range(CHUNKS)]
    move_all(
        [sources[0].at[p] for p in parts] + sources[1:], [targets[0].at[p] for p in parts] + targets[1:], refs[-1]
    )


HBM = pl.BlockSpec(memory_space=pltpu.HBM)


def stage(tiles, *scalars):
    return pl.pallas_call(
        stage_kernel,
        out_shape=[pltpu.VMEM(tiles.shape, tiles.dtype)] + [pltpu.SMEM(a.shape, a.dtype) for a in scalars],
        in_specs=[HBM] * (1 + len(scalars)),
        out_specs=[VMEM] + [SMEM] * len(scalars),
        scratch_shapes=[pltpu.SemaphoreType.DMA((CHUNKS + len(scalars),))],
        cost_estimate=pl.CostEstimate(flops=0, bytes_accessed=tiles.size * 4, transcendentals=0),
    )(tiles, *scalars)


def turn_kernel(tiles_ref, parts_ref):
    for t in range(tiles_ref.shape[1]):
        parts_ref[t, :, :TILE], parts_ref[t, :, TILE:] = split(tiles_ref[0, t].T)


def turn(tiles):
    slots = tiles.shape[1]
    parts = pltpu.VMEM((slots, TILE, 2 * TILE), jnp.bfloat16)
    return pl.pallas_call(
        turn_kernel,
        out_shape=[parts],
        in_specs=[VMEM],
        out_specs=[VMEM],
        compiler_params=pltpu.CompilerParams(vmem_limit_bytes=32 * 2**20),
        cost_estimate=pl.CostEstimate(flops=0, bytes_accessed=tiles.size * 8, transcendentals=0),
    )(tiles)


def products(slots, width, count_ref, from_ref, to_ref, seg_ref, parts_of, out_ref):
    out_ref[...] = jnp.zeros_like(out_ref)
    for t in range(slots):
        vec = jnp.where(t < count_ref[0, 0], seg_ref[from_ref[0, t]], 0.0)
        hi = vec.astype(jnp.bfloat16).astype(jnp.float32)
        both = jnp.concatenate([hi, vec - hi], axis=0).astype(jnp.bfloat16)
        got = jnp.dot(both, parts_of(t), preferred_element_type=jnp.float32)
        to = to_ref[0, t]
        out_ref[to] = out_ref[to] + (got[:width, :TILE] + (got[width:, :TILE] + got[:width, TILE:]))


def mirror_kernel(count_ref, rows_ref, cols_ref, seg_ref, tiles_ref, out_ref):
    slots, width = tiles_ref.shape[1], seg_ref.shape[1]
    products(slots, width, count_ref, rows_ref, cols_ref, seg_ref, lambda t: jnp.concatenate(split(tiles_ref[0, t]), axis=1), out_ref)


def plain_kernel(count_ref, rows_ref, cols_ref, seg_ref, parts_ref, out_ref):
    slots, width = parts_ref.shape[0], seg_ref.shape[1]
    products(slots, width, count_ref, cols_ref, rows_ref, seg_ref, lambda t: parts_ref[t], out_ref)


def apply_tiles(kernel, counts, tile_rows, tile_cols, seg, *tiles):
    slots = tile_rows.shape[1]
    return pl.pallas_call(
        kernel,
        out_shape=jax.ShapeDtypeStruct(seg.shape, jnp.float32),
        in_specs=[SMEM] * 3 + [VMEM] * (1 + len(tiles)),
        out_specs=VMEM,
        compiler_params=pltpu.CompilerParams(vmem_limit_bytes=32 * 2**20),
        cost_estimate=pl.CostEstimate(
            flops=2 * 4 * slots * 8 * TILE * TILE, bytes_accessed=slots * TILE * TILE * 4, transcendentals=0
        ),
    )(counts, tile_rows, tile_cols, seg, *tiles)


def local(vectors, tiles, tile_rows, tile_cols, counts):
    nrow, ncol = lax.axis_size("row"), lax.axis_size("col")
    width, piece_len = vectors.shape
    per = piece_len // TILE

    def place(r, c):
        return (r % nrow) * ncol + c

    half = ncol // 2

    def other(c):
        return (c + half) % ncol

    def sender(s, c):
        return other(c) if c % half == 0 or s % 2 == 0 else c

    onward = [(place(r, sender(r, c)), place(r + c, c)) for r in range(nrow) for c in range(ncol)]
    backward = [(place(r + c, c), place(r, other(c))) for r in range(nrow) for c in range(ncol)]
    piece = vectors.reshape(width, per, TILE).transpose(1, 0, 2)
    tiles, tile_rows, tile_cols = stage(tiles, tile_rows, tile_cols)
    places = (counts, tile_rows, tile_cols)
    own = lax.all_to_all(jnp.broadcast_to(piece[None], (ncol, *piece.shape)), "col", split_axis=0, concat_axis=0, tiled=True)
    own_seg = own.reshape(ncol * per, width, TILE)
    other_seg = lax.ppermute(own_seg, AXES, onward)
    col_part = apply_tiles(mirror_kernel, *places, own_seg, tiles)
    home = lax.ppermute(col_part, AXES, backward)
    row_part = apply_tiles(plain_kernel, *places, other_seg, *turn(tiles))
    total = (row_part + home).reshape(ncol, per, width, TILE)
    pieces = lax.all_to_all(total, "col", split_axis=0, concat_axis=0, tiled=True)
    return pieces.sum(axis=0).transpose(1, 0, 2).reshape(width, piece_len)


def solution(mesh):
    placed = (
        P(None, AXES),
        P("row", "col", None, None),
        P("row", "col"),
        P("row", "col"),
        P("row", "col"),
    )
    return jax.shard_map(local, mesh=mesh, in_specs=placed, out_specs=P(None, AXES), check_vma=False)
```

```python
import functools

import jax
import jax.numpy as jnp
from jax import lax
from jax.experimental import pallas as pl
from jax.experimental.pallas import tpu as pltpu
from jax.sharding import PartitionSpec as P

TILE = 128
CHUNKS = 4
SWAPS = (10, 0, 10, 8)
AXES = ("row", "col")
SMEM = pl.BlockSpec(memory_space=pltpu.SMEM)
VMEM = pl.BlockSpec(memory_space=pltpu.VMEM)


def split(x):
    hi = x.astype(jnp.bfloat16)
    return hi, (x - hi.astype(jnp.float32)).astype(jnp.bfloat16)


def move_all(sources, targets, sems):
    moves = [pltpu.make_async_copy(s, t, sems.at[n]) for n, (s, t) in enumerate(zip(sources, targets, strict=True))]
    for move in moves:
        move.start()
    for move in moves:
        move.wait()


def stage_kernel(*refs):
    half = len(refs) // 2
    sources, targets = list(refs[:half]), list(refs[half:-1])
    chunk = sources[0].shape[1] // CHUNKS
    parts = [(0, pl.ds(n * chunk, chunk)) for n in range(CHUNKS)]
    move_all(
        [sources[0].at[p] for p in parts] + sources[1:], [targets[0].at[p] for p in parts] + targets[1:], refs[-1]
    )


HBM = pl.BlockSpec(memory_space=pltpu.HBM)


def stage(tiles, *scalars):
    return pl.pallas_call(
        stage_kernel,
        out_shape=[pltpu.VMEM(tiles.shape, tiles.dtype)] + [pltpu.SMEM(a.shape, a.dtype) for a in scalars],
        in_specs=[HBM] * (1 + len(scalars)),
        out_specs=[VMEM] + [SMEM] * len(scalars),
        scratch_shapes=[pltpu.SemaphoreType.DMA((CHUNKS + len(scalars),))],
        cost_estimate=pl.CostEstimate(flops=0, bytes_accessed=tiles.size * 4, transcendentals=0),
    )(tiles, *scalars)


def turn_kernel(tiles_ref, parts_ref):
    for t in range(tiles_ref.shape[1]):
        parts_ref[t, :, :TILE], parts_ref[t, :, TILE:] = split(tiles_ref[0, t].T)


def turn(tiles):
    slots = tiles.shape[1]
    parts = pltpu.VMEM((slots, TILE, 2 * TILE), jnp.bfloat16)
    return pl.pallas_call(
        turn_kernel,
        out_shape=[parts],
        in_specs=[VMEM],
        out_specs=[VMEM],
        compiler_params=pltpu.CompilerParams(vmem_limit_bytes=32 * 2**20),
        cost_estimate=pl.CostEstimate(flops=0, bytes_accessed=tiles.size * 8, transcendentals=0),
    )(tiles)


def products(slots, width, count_ref, from_ref, to_ref, seg_ref, parts_of, out_ref):
    out_ref[...] = jnp.zeros_like(out_ref)
    for t in range(slots):
        vec = jnp.where(t < count_ref[0, 0], seg_ref[from_ref[0, t]], 0.0)
        hi = vec.astype(jnp.bfloat16).astype(jnp.float32)
        both = jnp.concatenate([hi, vec - hi], axis=0).astype(jnp.bfloat16)
        got = jnp.dot(both, parts_of(t), preferred_element_type=jnp.float32)
        to = to_ref[0, t]
        out_ref[to] = out_ref[to] + (got[:width, :TILE] + (got[width:, :TILE] + got[:width, TILE:]))


def mirror_kernel(count_ref, rows_ref, cols_ref, seg_ref, tiles_ref, out_ref):
    slots, width = tiles_ref.shape[1], seg_ref.shape[1]
    products(slots, width, count_ref, rows_ref, cols_ref, seg_ref, lambda t: jnp.concatenate(split(tiles_ref[0, t]), axis=1), out_ref)


def plain_kernel(count_ref, rows_ref, cols_ref, seg_ref, parts_ref, out_ref):
    slots, width = parts_ref.shape[0], seg_ref.shape[1]
    products(slots, width, count_ref, cols_ref, rows_ref, seg_ref, lambda t: parts_ref[t], out_ref)


def apply_tiles(kernel, counts, tile_rows, tile_cols, seg, *tiles):
    slots = tile_rows.shape[1]
    return pl.pallas_call(
        kernel,
        out_shape=jax.ShapeDtypeStruct(seg.shape, jnp.float32),
        in_specs=[SMEM] * 3 + [VMEM] * (1 + len(tiles)),
        out_specs=VMEM,
        compiler_params=pltpu.CompilerParams(vmem_limit_bytes=32 * 2**20),
        cost_estimate=pl.CostEstimate(
            flops=2 * 4 * slots * 8 * TILE * TILE, bytes_accessed=slots * TILE * TILE * 4, transcendentals=0
        ),
    )(counts, tile_rows, tile_cols, seg, *tiles)


def local(vectors, tiles, tile_rows, tile_cols, counts):
    nrow, ncol = lax.axis_size("row"), lax.axis_size("col")
    width, piece_len = vectors.shape
    per = piece_len // TILE

    def place(r, c):
        return (r % nrow) * ncol + c

    half = ncol // 2

    def other(c):
        return (c + half) % ncol

    def sender(s, c):
        return other(c) if c % half == 0 or SWAPS[s % 4] >> c % half & 1 else c

    onward = [(place(r, sender(r, c)), place(r + c, c)) for r in range(nrow) for c in range(ncol)]
    backward = [(place(r + c, c), place(r, other(c))) for r in range(nrow) for c in range(ncol)]
    piece = vectors.reshape(width, per, TILE).transpose(1, 0, 2)
    tiles, tile_rows, tile_cols = stage(tiles, tile_rows, tile_cols)
    places = (counts, tile_rows, tile_cols)
    own = lax.all_to_all(jnp.broadcast_to(piece[None], (ncol, *piece.shape)), "col", split_axis=0, concat_axis=0, tiled=True)
    own_seg = own.reshape(ncol * per, width, TILE)
    other_seg = lax.ppermute(own_seg, AXES, onward)
    col_part = apply_tiles(mirror_kernel, *places, own_seg, tiles)
    home = lax.ppermute(col_part, AXES, backward)
    row_part = apply_tiles(plain_kernel, *places, other_seg, *turn(tiles))
    total = (row_part + home).reshape(ncol, per, width, TILE)
    pieces = lax.all_to_all(total, "col", split_axis=0, concat_axis=0, tiled=True)
    return pieces.sum(axis=0).transpose(1, 0, 2).reshape(width, piece_len)


def solution(mesh):
    placed = (
        P(None, AXES),
        P("row", "col", None, None),
        P("row", "col"),
        P("row", "col"),
        P("row", "col"),
    )
    return jax.shard_map(local, mesh=mesh, in_specs=placed, out_specs=P(None, AXES), check_vma=False)
```

```python
import functools

import jax
import jax.numpy as jnp
from jax import lax
from jax.experimental import pallas as pl
from jax.experimental.pallas import tpu as pltpu
from jax.sharding import PartitionSpec as P

TILE = 128
CHUNKS = 4
SWAPS = (10, 0, 2, 8)
AXES = ("row", "col")
SMEM = pl.BlockSpec(memory_space=pltpu.SMEM)
VMEM = pl.BlockSpec(memory_space=pltpu.VMEM)


def split(x):
    hi = x.astype(jnp.bfloat16)
    return hi, (x - hi.astype(jnp.float32)).astype(jnp.bfloat16)


def move_all(sources, targets, sems):
    moves = [pltpu.make_async_copy(s, t, sems.at[n]) for n, (s, t) in enumerate(zip(sources, targets, strict=True))]
    for move in moves:
        move.start()
    for move in moves:
        move.wait()


def stage_kernel(*refs):
    half = len(refs) // 2
    sources, targets = list(refs[:half]), list(refs[half:-1])
    chunk = sources[0].shape[1] // CHUNKS
    parts = [(0, pl.ds(n * chunk, chunk)) for n in range(CHUNKS)]
    move_all(
        [sources[0].at[p] for p in parts] + sources[1:], [targets[0].at[p] for p in parts] + targets[1:], refs[-1]
    )


HBM = pl.BlockSpec(memory_space=pltpu.HBM)


def stage(tiles, *scalars):
    return pl.pallas_call(
        stage_kernel,
        out_shape=[pltpu.VMEM(tiles.shape, tiles.dtype)] + [pltpu.SMEM(a.shape, a.dtype) for a in scalars],
        in_specs=[HBM] * (1 + len(scalars)),
        out_specs=[VMEM] + [SMEM] * len(scalars),
        scratch_shapes=[pltpu.SemaphoreType.DMA((CHUNKS + len(scalars),))],
        cost_estimate=pl.CostEstimate(flops=0, bytes_accessed=tiles.size * 4, transcendentals=0),
    )(tiles, *scalars)


def turn_kernel(tiles_ref, parts_ref):
    for t in range(tiles_ref.shape[1]):
        parts_ref[t, :, :TILE], parts_ref[t, :, TILE:] = split(tiles_ref[0, t].T)


def turn(tiles):
    slots = tiles.shape[1]
    parts = pltpu.VMEM((slots, TILE, 2 * TILE), jnp.bfloat16)
    return pl.pallas_call(
        turn_kernel,
        out_shape=[parts],
        in_specs=[VMEM],
        out_specs=[VMEM],
        compiler_params=pltpu.CompilerParams(vmem_limit_bytes=32 * 2**20),
        cost_estimate=pl.CostEstimate(flops=0, bytes_accessed=tiles.size * 8, transcendentals=0),
    )(tiles)


def products(slots, width, count_ref, from_ref, to_ref, seg_ref, parts_of, out_ref):
    out_ref[...] = jnp.zeros_like(out_ref)
    for t in range(slots):
        vec = jnp.where(t < count_ref[0, 0], seg_ref[from_ref[0, t]], 0.0)
        hi = vec.astype(jnp.bfloat16).astype(jnp.float32)
        both = jnp.concatenate([hi, vec - hi], axis=0).astype(jnp.bfloat16)
        got = jnp.dot(both, parts_of(t), preferred_element_type=jnp.float32)
        to = to_ref[0, t]
        out_ref[to] = out_ref[to] + (got[:width, :TILE] + (got[width:, :TILE] + got[:width, TILE:]))


def mirror_kernel(count_ref, rows_ref, cols_ref, seg_ref, tiles_ref, out_ref):
    slots, width = tiles_ref.shape[1], seg_ref.shape[1]
    products(slots, width, count_ref, rows_ref, cols_ref, seg_ref, lambda t: jnp.concatenate(split(tiles_ref[0, t]), axis=1), out_ref)


def plain_kernel(count_ref, rows_ref, cols_ref, seg_ref, parts_ref, out_ref):
    slots, width = parts_ref.shape[0], seg_ref.shape[1]
    products(slots, width, count_ref, cols_ref, rows_ref, seg_ref, lambda t: parts_ref[t], out_ref)


def apply_tiles(kernel, counts, tile_rows, tile_cols, seg, *tiles):
    slots = tile_rows.shape[1]
    return pl.pallas_call(
        kernel,
        out_shape=jax.ShapeDtypeStruct(seg.shape, jnp.float32),
        in_specs=[SMEM] * 3 + [VMEM] * (1 + len(tiles)),
        out_specs=VMEM,
        compiler_params=pltpu.CompilerParams(vmem_limit_bytes=32 * 2**20),
        cost_estimate=pl.CostEstimate(
            flops=2 * 4 * slots * 8 * TILE * TILE, bytes_accessed=slots * TILE * TILE * 4, transcendentals=0
        ),
    )(counts, tile_rows, tile_cols, seg, *tiles)


def local(vectors, tiles, tile_rows, tile_cols, counts):
    nrow, ncol = lax.axis_size("row"), lax.axis_size("col")
    width, piece_len = vectors.shape
    per = piece_len // TILE

    def place(r, c):
        return (r % nrow) * ncol + c

    half = ncol // 2

    def other(c):
        return (c + half) % ncol

    def sender(s, c):
        return other(c) if c % half == 0 or SWAPS[s % 4] >> c % half & 1 else c

    onward = [(place(r, sender(r, c)), place(r + c, c)) for r in range(nrow) for c in range(ncol)]
    backward = [(place(r + c, c), place(r, other(c))) for r in range(nrow) for c in range(ncol)]
    piece = vectors.reshape(width, per, TILE).transpose(1, 0, 2)
    tiles, tile_rows, tile_cols = stage(tiles, tile_rows, tile_cols)
    places = (counts, tile_rows, tile_cols)
    own = lax.all_to_all(jnp.broadcast_to(piece[None], (ncol, *piece.shape)), "col", split_axis=0, concat_axis=0, tiled=True)
    own_seg = own.reshape(ncol * per, width, TILE)
    other_seg = lax.ppermute(own_seg, AXES, onward)
    col_part = apply_tiles(mirror_kernel, *places, own_seg, tiles)
    home = lax.ppermute(col_part, AXES, backward)
    row_part = apply_tiles(plain_kernel, *places, other_seg, *turn(tiles))
    total = (row_part + home).reshape(ncol, per, width, TILE)
    pieces = lax.all_to_all(total, "col", split_axis=0, concat_axis=0, tiled=True)
    return pieces.sum(axis=0).transpose(1, 0, 2).reshape(width, piece_len)


def solution(mesh):
    placed = (
        P(None, AXES),
        P("row", "col", None, None),
        P("row", "col"),
        P("row", "col"),
        P("row", "col"),
    )
    return jax.shard_map(local, mesh=mesh, in_specs=placed, out_specs=P(None, AXES), check_vma=False)
```

```python
import functools

import jax
import jax.numpy as jnp
from jax import lax
from jax.experimental import pallas as pl
from jax.experimental.pallas import tpu as pltpu
from jax.sharding import PartitionSpec as P

TILE = 128
CHUNKS = 4
SWAPS = (10, 2, 2, 10)
AXES = ("row", "col")
SMEM = pl.BlockSpec(memory_space=pltpu.SMEM)
VMEM = pl.BlockSpec(memory_space=pltpu.VMEM)


def split(x):
    hi = x.astype(jnp.bfloat16)
    return hi, (x - hi.astype(jnp.float32)).astype(jnp.bfloat16)


def move_all(sources, targets, sems):
    moves = [pltpu.make_async_copy(s, t, sems.at[n]) for n, (s, t) in enumerate(zip(sources, targets, strict=True))]
    for move in moves:
        move.start()
    for move in moves:
        move.wait()


def stage_kernel(*refs):
    half = len(refs) // 2
    sources, targets = list(refs[:half]), list(refs[half:-1])
    chunk = sources[0].shape[1] // CHUNKS
    parts = [(0, pl.ds(n * chunk, chunk)) for n in range(CHUNKS)]
    move_all(
        [sources[0].at[p] for p in parts] + sources[1:], [targets[0].at[p] for p in parts] + targets[1:], refs[-1]
    )


HBM = pl.BlockSpec(memory_space=pltpu.HBM)


def stage(tiles, *scalars):
    return pl.pallas_call(
        stage_kernel,
        out_shape=[pltpu.VMEM(tiles.shape, tiles.dtype)] + [pltpu.SMEM(a.shape, a.dtype) for a in scalars],
        in_specs=[HBM] * (1 + len(scalars)),
        out_specs=[VMEM] + [SMEM] * len(scalars),
        scratch_shapes=[pltpu.SemaphoreType.DMA((CHUNKS + len(scalars),))],
        cost_estimate=pl.CostEstimate(flops=0, bytes_accessed=tiles.size * 4, transcendentals=0),
    )(tiles, *scalars)


def turn_kernel(tiles_ref, parts_ref):
    for t in range(tiles_ref.shape[1]):
        parts_ref[t, :, :TILE], parts_ref[t, :, TILE:] = split(tiles_ref[0, t].T)


def turn(tiles):
    slots = tiles.shape[1]
    parts = pltpu.VMEM((slots, TILE, 2 * TILE), jnp.bfloat16)
    return pl.pallas_call(
        turn_kernel,
        out_shape=[parts],
        in_specs=[VMEM],
        out_specs=[VMEM],
        compiler_params=pltpu.CompilerParams(vmem_limit_bytes=32 * 2**20),
        cost_estimate=pl.CostEstimate(flops=0, bytes_accessed=tiles.size * 8, transcendentals=0),
    )(tiles)


def products(slots, width, count_ref, from_ref, to_ref, seg_ref, parts_of, out_ref):
    out_ref[...] = jnp.zeros_like(out_ref)
    for t in range(slots):
        vec = jnp.where(t < count_ref[0, 0], seg_ref[from_ref[0, t]], 0.0)
        hi = vec.astype(jnp.bfloat16).astype(jnp.float32)
        both = jnp.concatenate([hi, vec - hi], axis=0).astype(jnp.bfloat16)
        got = jnp.dot(both, parts_of(t), preferred_element_type=jnp.float32)
        to = to_ref[0, t]
        out_ref[to] = out_ref[to] + (got[:width, :TILE] + (got[width:, :TILE] + got[:width, TILE:]))


def mirror_kernel(count_ref, rows_ref, cols_ref, seg_ref, tiles_ref, out_ref):
    slots, width = tiles_ref.shape[1], seg_ref.shape[1]
    products(slots, width, count_ref, rows_ref, cols_ref, seg_ref, lambda t: jnp.concatenate(split(tiles_ref[0, t]), axis=1), out_ref)


def plain_kernel(count_ref, rows_ref, cols_ref, seg_ref, parts_ref, out_ref):
    slots, width = parts_ref.shape[0], seg_ref.shape[1]
    products(slots, width, count_ref, cols_ref, rows_ref, seg_ref, lambda t: parts_ref[t], out_ref)


def apply_tiles(kernel, counts, tile_rows, tile_cols, seg, *tiles):
    slots = tile_rows.shape[1]
    return pl.pallas_call(
        kernel,
        out_shape=jax.ShapeDtypeStruct(seg.shape, jnp.float32),
        in_specs=[SMEM] * 3 + [VMEM] * (1 + len(tiles)),
        out_specs=VMEM,
        compiler_params=pltpu.CompilerParams(vmem_limit_bytes=32 * 2**20),
        cost_estimate=pl.CostEstimate(
            flops=2 * 4 * slots * 8 * TILE * TILE, bytes_accessed=slots * TILE * TILE * 4, transcendentals=0
        ),
    )(counts, tile_rows, tile_cols, seg, *tiles)


def local(vectors, tiles, tile_rows, tile_cols, counts):
    nrow, ncol = lax.axis_size("row"), lax.axis_size("col")
    width, piece_len = vectors.shape
    per = piece_len // TILE

    def place(r, c):
        return (r % nrow) * ncol + c

    half = ncol // 2

    def other(c):
        return (c + half) % ncol

    def sender(s, c):
        return other(c) if c % half == 0 or SWAPS[s % 4] >> c % half & 1 else c

    onward = [(place(r, sender(r, c)), place(r + c, c)) for r in range(nrow) for c in range(ncol)]
    backward = [(place(r + c, c), place(r, other(c))) for r in range(nrow) for c in range(ncol)]
    piece = vectors.reshape(width, per, TILE).transpose(1, 0, 2)
    tiles, tile_rows, tile_cols = stage(tiles, tile_rows, tile_cols)
    places = (counts, tile_rows, tile_cols)
    own = lax.all_to_all(jnp.broadcast_to(piece[None], (ncol, *piece.shape)), "col", split_axis=0, concat_axis=0, tiled=True)
    own_seg = own.reshape(ncol * per, width, TILE)
    other_seg = lax.ppermute(own_seg, AXES, onward)
    col_part = apply_tiles(mirror_kernel, *places, own_seg, tiles)
    home = lax.ppermute(col_part, AXES, backward)
    row_part = apply_tiles(plain_kernel, *places, other_seg, *turn(tiles))
    total = (row_part + home).reshape(ncol, per, width, TILE)
    pieces = lax.all_to_all(total, "col", split_axis=0, concat_axis=0, tiled=True)
    return pieces.sum(axis=0).transpose(1, 0, 2).reshape(width, piece_len)


def solution(mesh):
    placed = (
        P(None, AXES),
        P("row", "col", None, None),
        P("row", "col"),
        P("row", "col"),
        P("row", "col"),
    )
    return jax.shard_map(local, mesh=mesh, in_specs=placed, out_specs=P(None, AXES), check_vma=False)
```

```python
import functools

import jax
import jax.numpy as jnp
from jax import lax
from jax.experimental import pallas as pl
from jax.experimental.pallas import tpu as pltpu
from jax.sharding import PartitionSpec as P

TILE = 128
CHUNKS = 1
SWAPS = (10, 2, 2, 10)
AXES = ("row", "col")
SMEM = pl.BlockSpec(memory_space=pltpu.SMEM)
VMEM = pl.BlockSpec(memory_space=pltpu.VMEM)


def split(x):
    hi = x.astype(jnp.bfloat16)
    return hi, (x - hi.astype(jnp.float32)).astype(jnp.bfloat16)


def move_all(sources, targets, sems):
    moves = [pltpu.make_async_copy(s, t, sems.at[n]) for n, (s, t) in enumerate(zip(sources, targets, strict=True))]
    for move in moves:
        move.start()
    for move in moves:
        move.wait()


def stage_kernel(*refs):
    half = len(refs) // 2
    sources, targets = list(refs[:half]), list(refs[half:-1])
    chunk = sources[0].shape[1] // CHUNKS
    parts = [(0, pl.ds(n * chunk, chunk)) for n in range(CHUNKS)]
    move_all(
        [sources[0].at[p] for p in parts] + sources[1:], [targets[0].at[p] for p in parts] + targets[1:], refs[-1]
    )


HBM = pl.BlockSpec(memory_space=pltpu.HBM)


def stage(tiles, *scalars):
    return pl.pallas_call(
        stage_kernel,
        out_shape=[pltpu.VMEM(tiles.shape, tiles.dtype)] + [pltpu.SMEM(a.shape, a.dtype) for a in scalars],
        in_specs=[HBM] * (1 + len(scalars)),
        out_specs=[VMEM] + [SMEM] * len(scalars),
        scratch_shapes=[pltpu.SemaphoreType.DMA((CHUNKS + len(scalars),))],
        cost_estimate=pl.CostEstimate(flops=0, bytes_accessed=tiles.size * 4, transcendentals=0),
    )(tiles, *scalars)


def turn_kernel(tiles_ref, parts_ref):
    for t in range(tiles_ref.shape[1]):
        parts_ref[t, :, :TILE], parts_ref[t, :, TILE:] = split(tiles_ref[0, t].T)


def turn(tiles):
    slots = tiles.shape[1]
    parts = pltpu.VMEM((slots, TILE, 2 * TILE), jnp.bfloat16)
    return pl.pallas_call(
        turn_kernel,
        out_shape=[parts],
        in_specs=[VMEM],
        out_specs=[VMEM],
        compiler_params=pltpu.CompilerParams(vmem_limit_bytes=32 * 2**20),
        cost_estimate=pl.CostEstimate(flops=0, bytes_accessed=tiles.size * 8, transcendentals=0),
    )(tiles)


def products(slots, width, count_ref, from_ref, to_ref, seg_ref, parts_of, out_ref):
    out_ref[...] = jnp.zeros_like(out_ref)
    for t in range(slots):
        vec = jnp.where(t < count_ref[0, 0], seg_ref[from_ref[0, t]], 0.0)
        hi = vec.astype(jnp.bfloat16).astype(jnp.float32)
        both = jnp.concatenate([hi, vec - hi], axis=0).astype(jnp.bfloat16)
        got = jnp.dot(both, parts_of(t), preferred_element_type=jnp.float32)
        to = to_ref[0, t]
        out_ref[to] = out_ref[to] + (got[:width, :TILE] + (got[width:, :TILE] + got[:width, TILE:]))


def mirror_kernel(count_ref, rows_ref, cols_ref, seg_ref, tiles_ref, out_ref):
    slots, width = tiles_ref.shape[1], seg_ref.shape[1]
    products(slots, width, count_ref, rows_ref, cols_ref, seg_ref, lambda t: jnp.concatenate(split(tiles_ref[0, t]), axis=1), out_ref)


def plain_kernel(count_ref, rows_ref, cols_ref, seg_ref, parts_ref, out_ref):
    slots, width = parts_ref.shape[0], seg_ref.shape[1]
    products(slots, width, count_ref, cols_ref, rows_ref, seg_ref, lambda t: parts_ref[t], out_ref)


def apply_tiles(kernel, counts, tile_rows, tile_cols, seg, *tiles):
    slots = tile_rows.shape[1]
    return pl.pallas_call(
        kernel,
        out_shape=jax.ShapeDtypeStruct(seg.shape, jnp.float32),
        in_specs=[SMEM] * 3 + [VMEM] * (1 + len(tiles)),
        out_specs=VMEM,
        compiler_params=pltpu.CompilerParams(vmem_limit_bytes=32 * 2**20),
        cost_estimate=pl.CostEstimate(
            flops=2 * 4 * slots * 8 * TILE * TILE, bytes_accessed=slots * TILE * TILE * 4, transcendentals=0
        ),
    )(counts, tile_rows, tile_cols, seg, *tiles)


def local(vectors, tiles, tile_rows, tile_cols, counts):
    nrow, ncol = lax.axis_size("row"), lax.axis_size("col")
    width, piece_len = vectors.shape
    per = piece_len // TILE

    def place(r, c):
        return (r % nrow) * ncol + c

    half = ncol // 2

    def other(c):
        return (c + half) % ncol

    def sender(s, c):
        return other(c) if c % half == 0 or SWAPS[s % 4] >> c % half & 1 else c

    onward = [(place(r, sender(r, c)), place(r + c, c)) for r in range(nrow) for c in range(ncol)]
    backward = [(place(r + c, c), place(r, other(c))) for r in range(nrow) for c in range(ncol)]
    piece = vectors.reshape(width, per, TILE).transpose(1, 0, 2)
    tiles, tile_rows, tile_cols = stage(tiles, tile_rows, tile_cols)
    places = (counts, tile_rows, tile_cols)
    own = lax.all_to_all(jnp.broadcast_to(piece[None], (ncol, *piece.shape)), "col", split_axis=0, concat_axis=0, tiled=True)
    own_seg = own.reshape(ncol * per, width, TILE)
    other_seg = lax.ppermute(own_seg, AXES, onward)
    col_part = apply_tiles(mirror_kernel, *places, own_seg, tiles)
    home = lax.ppermute(col_part, AXES, backward)
    row_part = apply_tiles(plain_kernel, *places, other_seg, *turn(tiles))
    total = (row_part + home).reshape(ncol, per, width, TILE)
    pieces = lax.all_to_all(total, "col", split_axis=0, concat_axis=0, tiled=True)
    return pieces.sum(axis=0).transpose(1, 0, 2).reshape(width, piece_len)


def solution(mesh):
    placed = (
        P(None, AXES),
        P("row", "col", None, None),
        P("row", "col"),
        P("row", "col"),
        P("row", "col"),
    )
    return jax.shard_map(local, mesh=mesh, in_specs=placed, out_specs=P(None, AXES), check_vma=False)
```
